32 devices in a mesh: groups: 2 (over y), job: 4 (over x, core), tensor: 4 (over z).
Axes of the slice: x: 2, y: 2, z: 4, core: 2. Of those that a mesh axis runs over, the one named last changes fastest.
Arguments:
- tokens: bfloat16 [16384, 8192], P(('groups', 'job'), 'tensor'), parts along dimension 0, may hold values from -6 to 6
- weight: bfloat16 [8192, 1024], P('tensor'), may hold values from -0.0625 to 0.0625
- dequant_scale: float32 [1024], P('tensor'), may hold values from 0.5 to 4
- down_factor: bfloat16 [32, 64, 8192], P(('groups', 'job'), None, 'tensor'), parts along dimension 0, may hold values from -0.0625 to 0.0625
- up_factor: bfloat16 [32, 64, 1024], P(('groups', 'job'), None, 'tensor'), parts along dimension 0, may hold values from -0.75 to 0.75
- counts: int32 [32], P(('groups', 'job')), parts along dimension 0, may hold values from 1 to 2045, as said below
- job_adapter: int32 [32], P(('groups', 'job')), parts along dimension 0, may hold values from 0 to 3
- cotangent: bfloat16 [16384, 1024], P(('groups', 'job'), 'tensor'), parts along dimension 0, may hold values from -6 to 6
Outputs:
- mixed: bfloat16 [16384, 1024], P(('groups', 'job'), 'tensor'), parts along dimension 0
- token_gradient: bfloat16 [16384, 8192], P(('groups', 'job'), 'tensor'), parts along dimension 0
- down_gradient: float32 [32, 64, 8192], P(('groups', 'job'), None, 'tensor'), parts along dimension 0
- up_gradient: float32 [32, 64, 1024], P(('groups', 'job'), None, 'tensor'), parts along dimension 0
The draws below stay inside these ranges and needn't reach their ends.
There are 2 independent parts, one for each index of `groups`. The reference program is written for one: setup_inputs(seed, part) draws one part's arguments, and reference() takes and returns one part's arrays. A program takes and returns all parts, laid end to end along the dimension named above; an argument that names none is the same for every part. Nothing has to cross between parts.
Inputs may be any that keep to these rules, and one draw needn't show every extreme that they name: Each count is 1 or more; the 4 counts of one index of job sum to at most 2048, and at some index of job to exactly 2048.
All inputs are finite; a program needn't handle non-finite values.
Results may differ from the reference program's by a relative error of at most 0.013.
Values may be sent and summed in bfloat16 or wider, within the bound.
A program may use at most 128 MiB of HBM per device.

```python
import math
import jax
import jax.numpy as jnp
from jax import lax

D = 8192
KV = 1024
R = 64
JOB_DEV = 4
ROWS_DEV = 2048
TOKENS = 8192
JOBS = 16
N_JOB = 4
N_TENSOR = 4


def draw_counts(key, part):
    key = jax.random.fold_in(key, 11)
    indices = JOBS // JOB_DEV
    first, second, third, fourth = jax.random.split(key, 4)
    left = jax.random.randint(first, (indices,), 1, ROWS_DEV + 1)
    right = jax.random.randint(second, (indices,), 1, ROWS_DEV + 1)
    totals = jnp.maximum(1 + left * right // ROWS_DEV, JOB_DEV)
    fullest = jax.random.randint(third, (), 0, indices)
    is_full = jnp.arange(indices) == fullest
    totals = jnp.where(is_full, ROWS_DEV, totals)
    shares = jax.random.randint(fourth, (indices, JOB_DEV), 1, 9)
    leading = (jnp.arange(JOB_DEV) == 0).astype(shares.dtype)
    shares = jnp.where(is_full[:, None], leading[None, :], shares)
    spare = totals - JOB_DEV
    cuts = jnp.cumsum(shares, axis=1)
    marks = spare[:, None] * cuts // cuts[:, -1:]
    before = jnp.concatenate([jnp.zeros((indices, 1), marks.dtype), marks[:, :-1]], axis=1)
    sizes = 1 + marks - before
    return sizes.reshape(-1).astype(jnp.int32)


def with_ends(values, key, low, high):
    extent = values.shape
    index_at = [jax.random.randint(jax.random.fold_in(key, axis), (), 0, extent[axis]) for axis in range(len(extent))]
    values = values.at[tuple(index_at)].set(low)
    longest = extent.index(max(extent))
    index_at[longest] = (index_at[longest] + 1) % extent[longest]
    return values.at[tuple(index_at)].set(high)


def block_scale(key, dims, cuts, least, top_value):
    loudness, own = 1.0, jax.random.fold_in(key, 6)
    for axis_at, shards_of in cuts:
        draws = jnp.exp(jax.random.uniform(jax.random.fold_in(own, axis_at), (shards_of,), jnp.float32, least / len(cuts), top_value / len(cuts)))
        loudness = loudness * jnp.repeat(draws, dims[axis_at] // shards_of).reshape([-1 if axis == axis_at else 1 for axis in range(len(dims))])
    return loudness


def noise(own_key, dims, scale, bound, shards=(), held_as=jnp.bfloat16):
    values = jax.random.normal(own_key, dims, jnp.float32) * scale
    if len(shards) > 0:
        values = block_scale(own_key, dims, shards, -0.22, 0.18) * values
    return jnp.clip(values, min=-bound, max=bound).astype(held_as)


def setup_inputs(seed: int = 0, part: int = 0) -> dict:
    keys = jax.random.split(jax.random.key(seed), 9)
    own_keys = jax.random.split(jax.random.fold_in(keys[8], part), 9)
    tokens = noise(own_keys[0], (TOKENS, D), 1.0, 6.0, ((0, 4), (1, 4)))
    weight = noise(keys[1], (D, KV), D ** -0.5, 0.0625, ((0, 4),))
    dequant_scale = jnp.clip(jnp.exp(math.log(4.0) - 2.0794415 * jax.random.uniform(keys[2], (KV,), jnp.float32) ** block_scale(keys[2], (KV,), ((0, 4),), -0.2, 0.2)), 0.5, 4.0)
    down_factor = noise(own_keys[3], (JOBS, R, D), D ** -0.5, 0.0625, ((0, 4), (2, 4)))
    up_factor = noise(own_keys[4], (JOBS, R, KV), R ** -0.5, 0.75, ((0, 4), (2, 4)))
    counts = draw_counts(jax.random.fold_in(jax.random.fold_in(keys[8], part), 71), part)
    job_adapter = with_ends(jax.random.randint(own_keys[6], (JOBS,), 0, JOB_DEV), jax.random.fold_in(own_keys[6], 1), 0, JOB_DEV - 1).astype(jnp.int32)
    cotangent = noise(own_keys[7], (TOKENS, KV), 1.0, 6.0, ((0, 4), (1, 4)))
    return {"tokens": tokens, "weight": weight, "dequant_scale": dequant_scale, "down_factor": down_factor, "up_factor": up_factor, "counts": counts, "job_adapter": job_adapter, "cotangent": cotangent}


ADAPTER_SCALE = 2.0


def selection(count_row, adapt_row, token_rows):
    bounds = jnp.cumsum(count_row).astype(jnp.int32)
    starts = (bounds - count_row).astype(jnp.int32)
    position = jnp.arange(token_rows, dtype=jnp.int32)[:, None]
    owned = ((position >= starts[None, :]) & (position < bounds[None, :])).astype(jnp.float32)
    slots = jnp.arange(count_row.shape[0], dtype=jnp.int32)[None, :]
    table = (adapt_row[:, None] == slots).astype(jnp.float32)
    select = jnp.dot(owned, table, precision=lax.Precision.HIGHEST)
    return select, jnp.sum(owned, axis=1)


def split_sum(left, right, pieces):
    width = left.shape[1] // pieces
    total = jnp.zeros((left.shape[0], right.shape[1]), jnp.float32)
    for piece in range(pieces):
        part = jnp.dot(left[:, piece * width:(piece + 1) * width], right[piece * width:(piece + 1) * width], preferred_element_type=jnp.float32)
        part = lax.optimization_barrier(part.astype(jnp.bfloat16))
        total = total + part.astype(jnp.float32)
    return total


def reference(tokens, weight, dequant_scale, down_factor, up_factor, counts, job_adapter, cotangent):
    def one_index(group):
        input_rows, cot_rows, count_row, adapt_row, down_slots, up_slots = group
        select, active_mask = selection(count_row, adapt_row, ROWS_DEV)
        wide = jnp.repeat(select, R, axis=1)
        down_factor_table = down_slots.reshape(JOB_DEV * R, D)
        up_factor_table = up_slots.reshape(JOB_DEV * R, KV)
        base = split_sum(input_rows, weight, N_TENSOR)
        frozen_scaled = (base * dequant_scale[None, :]).astype(jnp.bfloat16)
        reduced_rows = (split_sum(input_rows, down_factor_table.T, N_TENSOR) * wide).astype(jnp.bfloat16)
        adapter_rows = jnp.dot(reduced_rows, up_factor_table, preferred_element_type=jnp.float32)
        mixed = ((frozen_scaled.astype(jnp.float32) + ADAPTER_SCALE * adapter_rows) * active_mask[:, None]).astype(jnp.bfloat16)
        masked_upstream = (cot_rows.astype(jnp.float32) * active_mask[:, None]).astype(jnp.bfloat16)
        gradient_rows = (split_sum(masked_upstream, up_factor_table.T, N_TENSOR) * wide).astype(jnp.bfloat16)
        scaled_cot = (cot_rows.astype(jnp.float32) * dequant_scale[None, :] * active_mask[:, None]).astype(jnp.bfloat16)
        frozen_gradient = jnp.dot(scaled_cot, weight.T, preferred_element_type=jnp.float32).astype(jnp.bfloat16)
        token_gradient = (frozen_gradient.astype(jnp.float32) + ADAPTER_SCALE * jnp.dot(gradient_rows, down_factor_table, preferred_element_type=jnp.float32)).astype(jnp.bfloat16)
        down_gradient = ADAPTER_SCALE * jnp.dot(gradient_rows.T, input_rows, preferred_element_type=jnp.float32)
        up_gradient = ADAPTER_SCALE * jnp.dot(reduced_rows.T, masked_upstream, preferred_element_type=jnp.float32)
        return mixed, token_gradient, down_gradient.reshape(JOB_DEV, R, D), up_gradient.reshape(JOB_DEV, R, KV)

    results = lax.map(one_index, (
        tokens.reshape(N_JOB, ROWS_DEV, D),
        cotangent.reshape(N_JOB, ROWS_DEV, KV),
        counts.reshape(N_JOB, JOB_DEV),
        job_adapter.reshape(N_JOB, JOB_DEV),
        down_factor.reshape(N_JOB, JOB_DEV, R, D),
        up_factor.reshape(N_JOB, JOB_DEV, R, KV)))
    return (results[0].reshape(TOKENS, KV), results[1].reshape(TOKENS, D), results[2].reshape(JOBS, R, D), results[3].reshape(JOBS, R, KV))
```

```python
import jax
import jax.numpy as jnp
from jax import lax
from jax.sharding import PartitionSpec as P

ADAPTER_SCALE = 2.0


def selection(counts, job_adapter, token_rows):
    bounds = jnp.cumsum(counts)
    starts = bounds - counts
    position = lax.broadcasted_iota(jnp.int32, (token_rows, 1), 0)
    owned = (position >= starts[None, :]) & (position < bounds[None, :])
    slot = jnp.sum(jnp.where(owned, job_adapter[None, :] + 1, 0), axis=1, keepdims=True) - 1
    return slot


def local(tokens, weight, dequant_scale, down_factor, up_factor, counts, job_adapter, cotangent):
    token_rows, width_portion = tokens.shape
    adapters, rank, _ = down_factor.shape
    out_part = up_factor.shape[2]
    cross = (((1,), (1,)), ((), ()))
    along_rows = (((0,), (0,)), ((), ()))
    slot = selection(counts, job_adapter, token_rows)
    live = slot >= 0
    down_table = down_factor.reshape(adapters * rank, width_portion)
    up_table = up_factor.reshape(adapters * rank, out_part)
    masked = jnp.where(live, cotangent, 0)
    scaled = jnp.where(live, cotangent.astype(jnp.float32) * dequant_scale[None, :], 0.0).astype(
        jnp.bfloat16
    )
    every = lax.all_gather(scaled, "tensor", axis=1, tiled=True)

    def own_slot(full):
        total = jnp.zeros((token_rows, rank), jnp.float32)
        for a in range(adapters):
            total = jnp.where(slot == a, full[:, a * rank : (a + 1) * rank], total)
        return total.astype(jnp.bfloat16)

    def spread(compact):
        return jnp.concatenate([jnp.where(slot == a, compact, 0) for a in range(adapters)], axis=1)

    low = own_slot(lax.dot_general(tokens, down_table, cross, preferred_element_type=jnp.float32))
    grad = own_slot(lax.dot_general(masked, up_table, cross, preferred_element_type=jnp.float32))
    both = lax.psum(jnp.concatenate([low, grad], axis=1), "tensor")
    low_rows = spread(both[:, :rank])
    grad_rows = spread(both[:, rank:])
    part = jnp.dot(tokens, weight, preferred_element_type=jnp.float32).astype(jnp.bfloat16)
    base = lax.psum_scatter(part, "tensor", scatter_dimension=1, tiled=True)
    back = lax.dot_general(every, weight, cross, preferred_element_type=jnp.float32)
    token_gradient = (
        back
        + ADAPTER_SCALE * jnp.dot(grad_rows, down_table, preferred_element_type=jnp.float32)
    ).astype(jnp.bfloat16)
    down_gradient = ADAPTER_SCALE * lax.dot_general(
        grad_rows, tokens, along_rows, preferred_element_type=jnp.float32
    )
    up_gradient = ADAPTER_SCALE * lax.dot_general(
        low_rows, masked, along_rows, preferred_element_type=jnp.float32
    )
    base_scaled = base.astype(jnp.float32) * dequant_scale[None, :]
    mixed = jnp.where(
        live,
        base_scaled
        + ADAPTER_SCALE * jnp.dot(low_rows, up_table, preferred_element_type=jnp.float32),
        0.0,
    ).astype(jnp.bfloat16)
    return (
        mixed,
        token_gradient,
        down_gradient.reshape(adapters, rank, width_portion),
        up_gradient.reshape(adapters, rank, out_part),
    )


def solution(mesh):
    placed = (
        P(("groups", "job"), "tensor"),
        P("tensor", None),
        P("tensor"),
        P(("groups", "job"), None, "tensor"),
        P(("groups", "job"), None, "tensor"),
        P(("groups", "job")),
        P(("groups", "job")),
        P(("groups", "job"), "tensor"),
    )
    return jax.shard_map(
        local,
        mesh=mesh,
        in_specs=placed,
        out_specs=(
            P(("groups", "job"), "tensor"),
            P(("groups", "job"), "tensor"),
            P(("groups", "job"), None, "tensor"),
            P(("groups", "job"), None, "tensor"),
        ),
        check_vma=False,
    )
```

```python
import functools

import jax
import jax.numpy as jnp
from jax import lax
from jax.experimental import pallas as pl
from jax.experimental.pallas import tpu as pltpu
from jax.sharding import PartitionSpec as P

ADAPTER_SCALE = 2.0
MACRO = 256
CHUNK = 64
LAG = 1
TILE = 512
F32 = jnp.float32
BF16 = jnp.bfloat16
CROSS = (((1,), (1,)), ((), ()))
ALONG = (((0,), (0,)), ((), ()))
MESH = pl.DeviceIdType.MESH


def own_slots(counts, job_adapter, token_rows):
    bounds = jnp.cumsum(counts)
    starts = bounds - counts
    position = lax.broadcasted_iota(jnp.int32, (token_rows, 1), 0)
    owned = (position >= starts[None, :]) & (position < bounds[None, :])
    return jnp.sum(jnp.where(owned, job_adapter[None, :] + 1, 0), axis=1, keepdims=True) - 1


def kernel(
    n,
    tokens_hbm,
    weight,
    scale,
    down,
    up,
    slot,
    cot,
    low_pick,
    grad_pick,
    lane_slot,
    mixed,
    grad_hbm,
    down_grad,
    up_grad,
    tokens,
    part,
    scaled,
    up_in,
    up_out,
    down_in,
    down_out,
    every,
    grad_buf,
    tok_sem,
    out_sem,
    up_send,
    up_recv,
    down_send,
    down_recv,
):
    me = lax.axis_index("tensor")
    rows_all, portion = tokens.shape
    width = weight.shape[1]
    own = scale.shape[1]
    macros = rows_all // MACRO
    chunks = rows_all // CHUNK
    per = MACRO // CHUNK
    last = n - 1

    def token_copy(m):
        span = pl.ds(pl.multiple_of(m * MACRO, MACRO), MACRO)
        return pltpu.make_async_copy(tokens_hbm.at[span], tokens.at[span], tok_sem.at[m])

    def out_copy(m):
        span = pl.ds(pl.multiple_of(m * MACRO, MACRO), MACRO)
        return pltpu.make_async_copy(grad_buf.at[span], grad_hbm.at[span], out_sem.at[m])

    def up_copy(c):
        span = pl.ds(pl.multiple_of(c * CHUNK, CHUNK), CHUNK)
        return pltpu.make_async_remote_copy(
            src_ref=up_out.at[span],
            dst_ref=up_in.at[span],
            send_sem=up_send.at[c],
            recv_sem=up_recv.at[c],
            device_id={"tensor": lax.rem(me + 1, n)},
            device_id_type=MESH,
        )

    def down_copy(c):
        span = pl.ds(pl.multiple_of(c * CHUNK, CHUNK), CHUNK)
        return pltpu.make_async_remote_copy(
            src_ref=down_out.at[span],
            dst_ref=down_in.at[span],
            send_sem=down_send.at[c],
            recv_sem=down_recv.at[c],
            device_id={"tensor": lax.rem(me + n - 1, n)},
            device_id_type=MESH,
        )

    for m in range(macros):
        token_copy(m).start()

    barrier = pltpu.get_barrier_semaphore()

    @pl.when(me > 0)
    def _():
        pl.semaphore_signal(
            barrier, inc=1, device_id={"tensor": lax.rem(me + n - 1, n)}, device_id_type=MESH
        )

    @pl.when(me < last)
    def _():
        pl.semaphore_signal(
            barrier, inc=1, device_id={"tensor": lax.rem(me + 1, n)}, device_id_type=MESH
        )

    inner = (me > 0) & (me < last)

    @pl.when(inner)
    def _():
        pl.semaphore_wait(barrier, 2)

    @pl.when(jnp.logical_not(inner))
    def _():
        pl.semaphore_wait(barrier, 1)

    down_grad[...] = jnp.zeros_like(down_grad)
    up_grad[...] = jnp.zeros_like(up_grad)

    def first_half(m):
        span = pl.ds(pl.multiple_of(m * MACRO, MACRO), MACRO)
        token_copy(m).wait()
        piece = tokens[span, :]
        where = slot[span, :]
        live = where >= 0
        mask = where == lane_slot[...]
        raw = jnp.where(live, cot[span, :].astype(F32), 0.0)
        scaled[span, :] = (raw * scale[...]).astype(BF16)
        low = lax.dot_general(piece, down[...], CROSS, preferred_element_type=F32)
        grad = lax.dot_general(raw.astype(BF16), up[...], CROSS, preferred_element_type=F32)
        low = jnp.where(mask, low, 0.0).astype(BF16)
        grad = jnp.where(mask, grad, 0.0).astype(BF16)
        packed = jnp.dot(low, low_pick[...], preferred_element_type=F32) + jnp.dot(
            grad, grad_pick[...], preferred_element_type=F32
        )
        part[span, width:] = packed.astype(BF16)

        @pl.loop(0, width // TILE)
        def _(j):
            cols = pl.ds(pl.multiple_of(j * TILE, TILE), TILE)
            part[span, cols] = jnp.dot(
                piece, weight[:, cols], preferred_element_type=F32
            ).astype(BF16)

    def relay(c, into, out, ahead, behind):
        span = pl.ds(pl.multiple_of(c * CHUNK, CHUNK), CHUNK)
        for j in range(n):
            cols = slice(j * own, (j + 1) * own)
            came = into[span, cols].astype(F32)
            mine = part[span, cols].astype(F32)
            value = jnp.where(
                behind(j), came, jnp.where(ahead(j), came + mine, scaled[span, :].astype(F32))
            )
            out[span, cols] = value.astype(BF16)
        out[span, width:] = (
            into[span, width:].astype(F32) + part[span, width:].astype(F32)
        ).astype(BF16)

    def second_half(m):
        span = pl.ds(pl.multiple_of(m * MACRO, MACRO), MACRO)
        where = slot[span, :]
        live = where >= 0
        mask = where == lane_slot[...]
        raw = jnp.where(live, cot[span, :], jnp.zeros((), BF16))
        packed = (
            up_in[span, width:].astype(F32)
            + down_in[span, width:].astype(F32)
            + part[span, width:].astype(F32)
        ).astype(BF16)
        low = jnp.where(
            mask, lax.dot_general(packed, low_pick[...], CROSS, preferred_element_type=F32), 0.0
        ).astype(BF16)
        grad = jnp.where(
            mask, lax.dot_general(packed, grad_pick[...], CROSS, preferred_element_type=F32), 0.0
        ).astype(BF16)
        base = jnp.zeros((MACRO, own), F32)
        for j in range(n):
            cols = slice(j * own, (j + 1) * own)
            above = down_in[span, cols].astype(F32)
            below = up_in[span, cols].astype(F32)
            mine = part[span, cols].astype(F32)
            base = jnp.where(j == me, above + below + mine, base)
            every[:, cols] = jnp.where(
                j < me, below, jnp.where(j > me, above, scaled[span, :].astype(F32))
            ).astype(BF16)
        term = jnp.dot(low, up[...], preferred_element_type=F32)
        value = (base * scale[...]).astype(BF16).astype(F32) + ADAPTER_SCALE * term
        mixed[span, :] = jnp.where(live, value, 0.0).astype(BF16)
        up_grad[...] += ADAPTER_SCALE * lax.dot_general(
            low, raw, ALONG, preferred_element_type=F32
        )

        @pl.loop(0, portion // TILE)
        def _(j):
            cols = pl.ds(pl.multiple_of(j * TILE, TILE), TILE)
            back = lax.dot_general(every[...], weight[cols, :], CROSS, preferred_element_type=F32)
            term = jnp.dot(grad, down[:, cols], preferred_element_type=F32)
            grad_buf[span, cols] = (
                back.astype(BF16).astype(F32) + ADAPTER_SCALE * term
            ).astype(BF16)
            down_grad[:, cols] += ADAPTER_SCALE * lax.dot_general(
                grad, tokens[span, cols], ALONG, preferred_element_type=F32
            )

        out_copy(m).start()

    tail = 1 + LAG * last

    @pl.loop(0, chunks + tail)
    def _(k):
        c_up = k - 1 - LAG * me
        c_down = k - 1 - LAG * (last - me)

        @pl.when((c_up >= 0) & (c_up < chunks))
        def _():
            @pl.when(me > 0)
            def _():
                up_copy(c_up).wait_recv()

            @pl.when(me == 0)
            def _():
                span = pl.ds(pl.multiple_of(c_up * CHUNK, CHUNK), CHUNK)
                up_in[span, :] = jnp.zeros((CHUNK, up_in.shape[1]), BF16)

            @pl.when(me < last)
            def _():
                relay(c_up, up_in, up_out, lambda j: j > me, lambda j: j < me)
                up_copy(c_up).start()

        @pl.when((c_down >= 0) & (c_down < chunks))
        def _():
            @pl.when(me < last)
            def _():
                down_copy(c_down).wait_recv()

            @pl.when(me == last)
            def _():
                span = pl.ds(pl.multiple_of(c_down * CHUNK, CHUNK), CHUNK)
                down_in[span, :] = jnp.zeros((CHUNK, down_in.shape[1]), BF16)

            @pl.when(me > 0)
            def _():
                relay(c_down, down_in, down_out, lambda j: j < me, lambda j: j > me)
                down_copy(c_down).start()

        @pl.when((lax.rem(k, per) == 0) & (k < chunks))
        def _():
            first_half(lax.div(k, per))

        done = k - tail + 1

        @pl.when((done > 0) & (lax.rem(jnp.maximum(done, 0), per) == 0))
        def _():
            second_half(lax.div(done, per) - 1)

    @pl.loop(0, chunks)
    def _(c):
        @pl.when(me < last)
        def _():
            up_copy(c).wait_send()

        @pl.when(me > 0)
        def _():
            down_copy(c).wait_send()

    @pl.loop(0, macros)
    def _(m):
        out_copy(m).wait()


def local(tokens, weight, dequant_scale, down_factor, up_factor, counts, job_adapter, cotangent):
    n = lax.axis_size("tensor")
    token_rows, portion = tokens.shape
    adapters, rank, _ = down_factor.shape
    out_part = up_factor.shape[2]
    width = weight.shape[1]
    slots = adapters * rank
    slot = own_slots(counts, job_adapter, token_rows)
    down_table = down_factor.reshape(slots, portion)
    up_table = up_factor.reshape(slots, out_part)
    line = jnp.arange(slots, dtype=jnp.int32)[:, None]
    lane = jnp.arange(2 * rank, dtype=jnp.int32)[None, :]
    low_pick = (line % rank == lane).astype(BF16)
    grad_pick = (line % rank + rank == lane).astype(BF16)
    lane_slot = (jnp.arange(slots, dtype=jnp.int32) // rank)[None, :]
    message = width + 2 * rank
    chunks = token_rows // CHUNK
    macros = token_rows // MACRO
    vmem = pl.BlockSpec(memory_space=pltpu.VMEM)
    hbm = pl.BlockSpec(memory_space=pl.ANY)
    mixed, token_gradient, down_gradient, up_gradient = pl.pallas_call(
        functools.partial(kernel, n),
        out_shape=(
            jax.ShapeDtypeStruct((token_rows, out_part), BF16),
            jax.ShapeDtypeStruct((token_rows, portion), BF16),
            jax.ShapeDtypeStruct((slots, portion), F32),
            jax.ShapeDtypeStruct((slots, out_part), F32),
        ),
        in_specs=[hbm] + [vmem] * 9,
        out_specs=(vmem, hbm, vmem, vmem),
        scratch_shapes=[
            pltpu.VMEM((token_rows, portion), BF16),
            pltpu.VMEM((token_rows, message), BF16),
            pltpu.VMEM((token_rows, out_part), BF16),
            pltpu.VMEM((token_rows, message), BF16),
            pltpu.VMEM((token_rows, message), BF16),
            pltpu.VMEM((token_rows, message), BF16),
            pltpu.VMEM((token_rows, message), BF16),
            pltpu.VMEM((MACRO, width), BF16),
            pltpu.VMEM((token_rows, portion), BF16),
            pltpu.SemaphoreType.DMA((macros,)),
            pltpu.SemaphoreType.DMA((macros,)),
            pltpu.SemaphoreType.DMA((chunks,)),
            pltpu.SemaphoreType.DMA((chunks,)),
            pltpu.SemaphoreType.DMA((chunks,)),
            pltpu.SemaphoreType.DMA((chunks,)),
        ],
        compiler_params=pltpu.CompilerParams(
            collective_id=0, has_side_effects=True, vmem_limit_bytes=60 * 2**20
        ),
        cost_estimate=pl.CostEstimate(
            flops=4 * token_rows * portion * (width + slots), bytes_accessed=30 * 2**20,
            transcendentals=0,
        ),
    )(
        tokens,
        weight,
        dequant_scale[None, :],
        down_table,
        up_table,
        slot,
        cotangent,
        low_pick,
        grad_pick,
        lane_slot,
    )
    return (
        mixed,
        token_gradient,
        down_gradient.reshape(adapters, rank, portion),
        up_gradient.reshape(adapters, rank, out_part),
    )


def solution(mesh):
    placed = (
        P(("groups", "job"), "tensor"),
        P("tensor", None),
        P("tensor"),
        P(("groups", "job"), None, "tensor"),
        P(("groups", "job"), None, "tensor"),
        P(("groups", "job")),
        P(("groups", "job")),
        P(("groups", "job"), "tensor"),
    )
    return jax.shard_map(
        local,
        mesh=mesh,
        in_specs=placed,
        out_specs=(
            P(("groups", "job"), "tensor"),
            P(("groups", "job"), "tensor"),
            P(("groups", "job"), None, "tensor"),
            P(("groups", "job"), None, "tensor"),
        ),
        check_vma=False,
    )
```

```python
import functools

import jax
import jax.numpy as jnp
import numpy as np
from jax import lax
from jax.experimental import pallas as pl
from jax.experimental.pallas import tpu as pltpu
from jax.sharding import PartitionSpec as P

ADAPTER_SCALE = 2.0
MACRO = 256
CHUNK = 64
LAG = 2
TILE = 512
F32 = jnp.float32
BF16 = jnp.bfloat16
CROSS = (((1,), (1,)), ((), ()))
ALONG = (((0,), (0,)), ((), ()))
MESH = pl.DeviceIdType.MESH


def kernel(
    n,
    tokens_hbm,
    weight,
    scale,
    down,
    up,
    counts,
    adapters,
    cot,
    low_pick,
    grad_pick,
    lane_slot,
    mixed,
    grad_hbm,
    down_grad,
    up_grad,
    tokens,
    part,
    scaled,
    up_in,
    up_out,
    down_in,
    down_out,
    every,
    grad_buf,
    tok_sem,
    out_sem,
    up_send,
    up_recv,
    down_send,
    down_recv,
):
    me = lax.axis_index("tensor")
    rows_all, portion = tokens.shape
    width = weight.shape[1]
    own = scale.shape[1]
    macros = rows_all // MACRO
    chunks = rows_all // CHUNK
    per = MACRO // CHUNK
    last = n - 1

    def own_slot(m):
        position = lax.broadcasted_iota(jnp.int32, (MACRO, 1), 0) + m * MACRO
        jobs = counts.shape[0]
        bounds = [counts[0]]
        for a in range(1, jobs):
            bounds.append(bounds[-1] + counts[a])
        found = jnp.full((MACRO, 1), -1, jnp.int32)
        for a in reversed(range(jobs)):
            found = jnp.where(position < bounds[a], adapters[a], found)
        return found

    def token_copy(m):
        span = pl.ds(pl.multiple_of(m * MACRO, MACRO), MACRO)
        return pltpu.make_async_copy(tokens_hbm.at[span], tokens.at[span], tok_sem.at[m])

    def out_copy(m):
        span = pl.ds(pl.multiple_of(m * MACRO, MACRO), MACRO)
        return pltpu.make_async_copy(grad_buf.at[span], grad_hbm.at[span], out_sem.at[m])

    def up_copy(c):
        span = pl.ds(pl.multiple_of(c * CHUNK, CHUNK), CHUNK)
        return pltpu.make_async_remote_copy(
            src_ref=up_out.at[span],
            dst_ref=up_in.at[span],
            send_sem=up_send.at[c],
            recv_sem=up_recv.at[c],
            device_id={"tensor": lax.rem(me + 1, n)},
            device_id_type=MESH,
        )

    def down_copy(c):
        span = pl.ds(pl.multiple_of(c * CHUNK, CHUNK), CHUNK)
        return pltpu.make_async_remote_copy(
            src_ref=down_out.at[span],
            dst_ref=down_in.at[span],
            send_sem=down_send.at[c],
            recv_sem=down_recv.at[c],
            device_id={"tensor": lax.rem(me + n - 1, n)},
            device_id_type=MESH,
        )

    for m in range(macros):
        token_copy(m).start()

    barrier = pltpu.get_barrier_semaphore()

    @pl.when(me > 0)
    def _():
        pl.semaphore_signal(
            barrier, inc=1, device_id={"tensor": lax.rem(me + n - 1, n)}, device_id_type=MESH
        )

    @pl.when(me < last)
    def _():
        pl.semaphore_signal(
            barrier, inc=1, device_id={"tensor": lax.rem(me + 1, n)}, device_id_type=MESH
        )

    inner = (me > 0) & (me < last)

    @pl.when(inner)
    def _():
        pl.semaphore_wait(barrier, 2)

    @pl.when(jnp.logical_not(inner))
    def _():
        pl.semaphore_wait(barrier, 1)

    down_grad[...] = jnp.zeros_like(down_grad)
    up_grad[...] = jnp.zeros_like(up_grad)

    def first_half(m):
        span = pl.ds(pl.multiple_of(m * MACRO, MACRO), MACRO)
        token_copy(m).wait()
        piece = tokens[span, :]
        where = own_slot(m)
        live = where >= 0
        mask = where == lane_slot[...]
        raw = jnp.where(live, cot[span, :].astype(F32), 0.0)
        scaled[span, :] = (raw * scale[...]).astype(BF16)
        low = lax.dot_general(piece, down[...], CROSS, preferred_element_type=F32)
        grad = lax.dot_general(raw.astype(BF16), up[...], CROSS, preferred_element_type=F32)
        low = jnp.where(mask, low, 0.0).astype(BF16)
        grad = jnp.where(mask, grad, 0.0).astype(BF16)
        packed = jnp.dot(low, low_pick[...], preferred_element_type=F32) + jnp.dot(
            grad, grad_pick[...], preferred_element_type=F32
        )
        part[span, width:] = packed.astype(BF16)

        @pl.loop(0, width // TILE)
        def _(j):
            cols = pl.ds(pl.multiple_of(j * TILE, TILE), TILE)
            part[span, cols] = jnp.dot(
                piece, weight[:, cols], preferred_element_type=F32
            ).astype(BF16)

    def relay(c, into, out, ahead, behind):
        span = pl.ds(pl.multiple_of(c * CHUNK, CHUNK), CHUNK)
        for j in range(n):
            cols = slice(j * own, (j + 1) * own)
            came = into[span, cols].astype(F32)
            mine = part[span, cols].astype(F32)
            value = jnp.where(
                behind(j), came, jnp.where(ahead(j), came + mine, scaled[span, :].astype(F32))
            )
            out[span, cols] = value.astype(BF16)
        out[span, width:] = (
            into[span, width:].astype(F32) + part[span, width:].astype(F32)
        ).astype(BF16)

    def second_half(m):
        span = pl.ds(pl.multiple_of(m * MACRO, MACRO), MACRO)
        where = own_slot(m)
        live = where >= 0
        mask = where == lane_slot[...]
        raw = jnp.where(live, cot[span, :], jnp.zeros((), BF16))
        packed = (
            up_in[span, width:].astype(F32)
            + down_in[span, width:].astype(F32)
            + part[span, width:].astype(F32)
        ).astype(BF16)
        low = jnp.where(
            mask, lax.dot_general(packed, low_pick[...], CROSS, preferred_element_type=F32), 0.0
        ).astype(BF16)
        grad = jnp.where(
            mask, lax.dot_general(packed, grad_pick[...], CROSS, preferred_element_type=F32), 0.0
        ).astype(BF16)
        base = jnp.zeros((MACRO, own), F32)
        for j in range(n):
            cols = slice(j * own, (j + 1) * own)
            above = down_in[span, cols].astype(F32)
            below = up_in[span, cols].astype(F32)
            mine = part[span, cols].astype(F32)
            base = jnp.where(j == me, above + below + mine, base)
            every[:, cols] = jnp.where(
                j < me, below, jnp.where(j > me, above, scaled[span, :].astype(F32))
            ).astype(BF16)
        term = jnp.dot(low, up[...], preferred_element_type=F32)
        value = (base * scale[...]).astype(BF16).astype(F32) + ADAPTER_SCALE * term
        mixed[span, :] = jnp.where(live, value, 0.0).astype(BF16)
        up_grad[...] += ADAPTER_SCALE * lax.dot_general(
            low, raw, ALONG, preferred_element_type=F32
        )

        @pl.loop(0, portion // TILE)
        def _(j):
            cols = pl.ds(pl.multiple_of(j * TILE, TILE), TILE)
            back = lax.dot_general(every[...], weight[cols, :], CROSS, preferred_element_type=F32)
            term = jnp.dot(grad, down[:, cols], preferred_element_type=F32)
            grad_buf[span, cols] = (
                back.astype(BF16).astype(F32) + ADAPTER_SCALE * term
            ).astype(BF16)
            down_grad[:, cols] += ADAPTER_SCALE * lax.dot_general(
                grad, tokens[span, cols], ALONG, preferred_element_type=F32
            )

        out_copy(m).start()

    tail = 1 + LAG * last

    @pl.loop(0, chunks + tail)
    def _(k):
        c_up = k - 1 - LAG * me
        c_down = k - 1 - LAG * (last - me)

        @pl.when((c_up >= 0) & (c_up < chunks))
        def _():
            @pl.when(me > 0)
            def _():
                up_copy(c_up).wait_recv()

            @pl.when(me == 0)
            def _():
                span = pl.ds(pl.multiple_of(c_up * CHUNK, CHUNK), CHUNK)
                up_in[span, :] = jnp.zeros((CHUNK, up_in.shape[1]), BF16)

            @pl.when(me < last)
            def _():
                relay(c_up, up_in, up_out, lambda j: j > me, lambda j: j < me)
                up_copy(c_up).start()

        @pl.when((c_down >= 0) & (c_down < chunks))
        def _():
            @pl.when(me < last)
            def _():
                down_copy(c_down).wait_recv()

            @pl.when(me == last)
            def _():
                span = pl.ds(pl.multiple_of(c_down * CHUNK, CHUNK), CHUNK)
                down_in[span, :] = jnp.zeros((CHUNK, down_in.shape[1]), BF16)

            @pl.when(me > 0)
            def _():
                relay(c_down, down_in, down_out, lambda j: j < me, lambda j: j > me)
                down_copy(c_down).start()

        @pl.when((lax.rem(k, per) == 0) & (k < chunks))
        def _():
            first_half(lax.div(k, per))

        done = k - tail + 1

        @pl.when((done > 0) & (lax.rem(jnp.maximum(done, 0), per) == 0))
        def _():
            second_half(lax.div(done, per) - 1)

    @pl.loop(0, chunks)
    def _(c):
        @pl.when(me < last)
        def _():
            up_copy(c).wait_send()

        @pl.when(me > 0)
        def _():
            down_copy(c).wait_send()

    @pl.loop(0, macros)
    def _(m):
        out_copy(m).wait()


def local(tokens, weight, dequant_scale, down_factor, up_factor, counts, job_adapter, cotangent):
    n = lax.axis_size("tensor")
    token_rows, portion = tokens.shape
    adapters, rank, _ = down_factor.shape
    out_part = up_factor.shape[2]
    width = weight.shape[1]
    slots = adapters * rank
    down_table = down_factor.reshape(slots, portion)
    up_table = up_factor.reshape(slots, out_part)
    line = np.arange(slots, dtype=np.int32)[:, None]
    lane = np.arange(2 * rank, dtype=np.int32)[None, :]
    low_pick = jnp.asarray((line % rank == lane).astype(BF16))
    grad_pick = jnp.asarray((line % rank + rank == lane).astype(BF16))
    lane_slot = jnp.asarray(line.T // rank)
    message = width + 2 * rank
    chunks = token_rows // CHUNK
    macros = token_rows // MACRO
    vmem = pl.BlockSpec(memory_space=pltpu.VMEM)
    smem = pl.BlockSpec(memory_space=pltpu.SMEM)
    hbm = pl.BlockSpec(memory_space=pl.ANY)
    mixed, token_gradient, down_gradient, up_gradient = pl.pallas_call(
        functools.partial(kernel, n),
        out_shape=(
            jax.ShapeDtypeStruct((token_rows, out_part), BF16),
            jax.ShapeDtypeStruct((token_rows, portion), BF16),
            jax.ShapeDtypeStruct((slots, portion), F32),
            jax.ShapeDtypeStruct((slots, out_part), F32),
        ),
        in_specs=[hbm] + [vmem] * 4 + [smem] * 2 + [vmem] * 4,
        out_specs=(vmem, hbm, vmem, vmem),
        scratch_shapes=[
            pltpu.VMEM((token_rows, portion), BF16),
            pltpu.VMEM((token_rows, message), BF16),
            pltpu.VMEM((token_rows, out_part), BF16),
            pltpu.VMEM((token_rows, message), BF16),
            pltpu.VMEM((token_rows, message), BF16),
            pltpu.VMEM((token_rows, message), BF16),
            pltpu.VMEM((token_rows, message), BF16),
            pltpu.VMEM((MACRO, width), BF16),
            pltpu.VMEM((token_rows, portion), BF16),
            pltpu.SemaphoreType.DMA((macros,)),
            pltpu.SemaphoreType.DMA((macros,)),
            pltpu.SemaphoreType.DMA((chunks,)),
            pltpu.SemaphoreType.DMA((chunks,)),
            pltpu.SemaphoreType.DMA((chunks,)),
            pltpu.SemaphoreType.DMA((chunks,)),
        ],
        compiler_params=pltpu.CompilerParams(
            collective_id=0, has_side_effects=True, vmem_limit_bytes=60 * 2**20
        ),
        cost_estimate=pl.CostEstimate(
            flops=4 * token_rows * portion * (width + slots), bytes_accessed=30 * 2**20,
            transcendentals=0,
        ),
    )(
        tokens,
        weight,
        dequant_scale[None, :],
        down_table,
        up_table,
        counts,
        job_adapter,
        cotangent,
        low_pick,
        grad_pick,
        lane_slot,
    )
    return (
        mixed,
        token_gradient,
        down_gradient.reshape(adapters, rank, portion),
        up_gradient.reshape(adapters, rank, out_part),
    )


def solution(mesh):
    placed = (
        P(("groups", "job"), "tensor"),
        P("tensor", None),
        P("tensor"),
        P(("groups", "job"), None, "tensor"),
        P(("groups", "job"), None, "tensor"),
        P(("groups", "job")),
        P(("groups", "job")),
        P(("groups", "job"), "tensor"),
    )
    return jax.shard_map(
        local,
        mesh=mesh,
        in_specs=placed,
        out_specs=(
            P(("groups", "job"), "tensor"),
            P(("groups", "job"), "tensor"),
            P(("groups", "job"), None, "tensor"),
            P(("groups", "job"), None, "tensor"),
        ),
        check_vma=False,
    )
```
